32 devices in a mesh: gx: 4 (over y, x), gy: 4 (over z), col: 2 (over core).
Axes of the slice: x: 2, y: 2, z: 4, core: 2. Of those that a mesh axis runs over, the one named last changes fastest.
Arguments:
- density: float32 [10, 10, 10, 16, 512], P('col', None, None, 'gx', 'gy'), may hold values from -6 to 6
- velocity: float32 [2, 16, 512], P(None, 'gx', 'gy'), may hold values from -3 to 3
- shear_rates: float32 [4, 16, 512], P(None, 'gx', 'gy'), may hold values from -4 to 4
- hermite_matrix: float32 [10, 10], replicated, may hold values from -2 to 2
- laguerre_matrix: float32 [10, 10], replicated, may hold values from -2 to 2
- flow_first: float32 [4, 10, 10], replicated, may hold values from -2 to 2
- flow_second: float32 [4, 10, 10], replicated, may hold values from -2 to 2
- stress_weights: float32 [3, 10, 10, 10], P(None, 'col'), may hold values from -0.1875 to 0.1875
Outputs:
- advanced: float32 [10, 10, 10, 16, 512], P('col', None, None, 'gx', 'gy')
- stress: float32 [3, 16, 512], P(None, 'gx', 'gy')
The draws below stay inside these ranges and needn't reach their ends.
All inputs are finite; a program needn't handle non-finite values.
Results may differ from the reference program's by a relative error of at most 0.0003.
Values sent between devices are 32-bit elements; how exact they have to be, the bound alone decides.
A program may use at most 128 MiB of HBM per device.

```python
import jax
import jax.numpy as jnp
from jax import lax

HM = 10
LM = 10
NX = 16
NY = 512


def levels(stream_key, shape, shards, least, top_value):
    def one(position, parts):
        draws = jax.random.uniform(jax.random.fold_in(jax.random.fold_in(stream_key, 6), position), (parts,), jnp.float32, least / len(shards), top_value / len(shards))
        return jnp.repeat(jnp.exp(draws), shape[position] // parts).reshape((-1,) + (1,) * (len(shape) - position - 1))

    level = one(*shards[0])
    for cut in shards[1:]:
        level = level * one(*cut)
    return level


def gaussian(rng, dims, scale, most, shards=(), kind=jnp.bfloat16):
    entries = scale * jax.random.normal(rng, dims, jnp.float32)
    if shards:
        entries = entries * levels(rng, dims, shards, -0.22, 0.18)
    return jnp.clip(entries, -most, most).astype(kind)


def setup_inputs(seed: int = 0) -> dict:
    streams_of = jax.random.split(jax.random.key(seed), 9)
    return {
        "density": gaussian(streams_of[0], (HM, HM, LM, NX, NY), 1.0, 6.0, ((0, 2), (3, 4), (4, 4)), jnp.float32),
        "velocity": gaussian(streams_of[1], (2, NX, NY), 1.0, 3.0, ((1, 4), (2, 4)), jnp.float32),
        "shear_rates": gaussian(streams_of[2], (4, NX, NY), 1.0, 4.0, ((1, 4), (2, 4)), jnp.float32),
        "hermite_matrix": gaussian(streams_of[3], (HM, HM), HM ** -0.5, 2.0, (), jnp.float32),
        "laguerre_matrix": gaussian(streams_of[4], (LM, LM), LM ** -0.5, 2.0, (), jnp.float32),
        "flow_first": gaussian(streams_of[5], (4, HM, HM), HM ** -0.5, 2.0, (), jnp.float32),
        "flow_second": gaussian(streams_of[6], (4, HM, HM), HM ** -0.5, 2.0, (), jnp.float32),
        "stress_weights": gaussian(streams_of[7], (3, HM, HM, LM), (HM * HM * LM) ** -0.5, 0.1875, ((1, 2),), jnp.float32),
    }


time_step = 0.1
highest = lax.Precision.HIGHEST


def stencil(minus_two, minus_one, center, plus_one, plus_two, speed):
    back = 1.5 * center - 2.0 * minus_one + 0.5 * minus_two
    front = -1.5 * center + 2.0 * plus_one - 0.5 * plus_two
    return speed * jnp.where(speed > 0, back, front)


def config_rate(center, gradient, hermite_matrix, laguerre_matrix, flow_first, flow_second):
    rate = jnp.einsum('ap,pqr...->aqr...', hermite_matrix, center, precision=highest)
    rate = rate + jnp.einsum('bq,pqr...->pbr...', hermite_matrix, center, precision=highest)
    rate = rate + jnp.einsum('cr,pqr...->pqc...', laguerre_matrix, center, precision=highest)
    for component in range(4):
        inner = jnp.einsum('bq,pqr...->pbr...', flow_second[component], center, precision=highest)
        outer = jnp.einsum('ap,pqr...->aqr...', flow_first[component], inner, precision=highest)
        rate = rate + gradient[component] * outer
    return rate


def reference(density, velocity, shear_rates, hermite_matrix, laguerre_matrix, flow_first, flow_second, stress_weights):
    offsets = jnp.arange(-2, 3, dtype=jnp.int32)
    positions = jnp.arange(NX, dtype=jnp.int32)

    def one_row(x_index):
        picked = ((x_index + offsets) % NX).astype(jnp.int32)
        rows = jnp.take(density, picked, axis=3)
        center = rows[:, :, :, 2, :]
        stream_speed = velocity[0, x_index]
        normal_speed = velocity[1, x_index]
        across = stencil(rows[:, :, :, 0, :], rows[:, :, :, 1, :], center, rows[:, :, :, 3, :], rows[:, :, :, 4, :], stream_speed)
        padded = jnp.pad(center, ((0, 0), (0, 0), (0, 0), (2, 2)))
        normal = stencil(padded[..., 0:NY], padded[..., 1:NY + 1], center, padded[..., 3:NY + 3], padded[..., 4:NY + 4], normal_speed)
        transport = across + normal
        gradient = shear_rates[:, x_index]
        rate = config_rate(center, gradient, hermite_matrix, laguerre_matrix, flow_first, flow_second)
        advanced_row = center + time_step * (rate - transport)
        stress_row = jnp.einsum('spqr,pqry->sy', stress_weights, advanced_row, precision=highest)
        return advanced_row, stress_row

    advanced_rows, stress_rows = lax.map(one_row, positions)
    advanced = jnp.moveaxis(advanced_rows, 0, 3)
    stress = jnp.moveaxis(stress_rows, 0, 1)
    return advanced, stress
```

```python
import functools

import jax
import jax.numpy as jnp
from jax import lax
from jax.experimental import pallas as pl
from jax.experimental.pallas import tpu as pltpu
from jax.sharding import PartitionSpec as P

time_step = 0.1
highest = lax.Precision.HIGHEST
MESH = pl.DeviceIdType.MESH

P_HERE = 5
HM = 10
QR = 100
WX = 4
WY = 128
ROWS = P_HERE * QR * WX
PQ = 56
GROUPS, PER = 10, 25
EARLY = 3


def dot(a, b):
    return jnp.dot(a, b, precision=highest, preferred_element_type=jnp.float32)


def tenth(i):
    return lax.shift_right_logical(i * 205, 11)


def iota(shape, axis):
    return lax.broadcasted_iota(jnp.int32, shape, axis)


def one(cond):
    return jnp.where(cond, 1.0, 0.0).astype(jnp.float32)


def kernel(nx, ny, dens_hbm, vel, shear, herm, lag, ff, fs, sw, out_hbm, stress_out,
           dens, other, acc, send_lo, send_hi, recv_lo, recv_hi, rim, rim_lo, rim_hi,
           xs, wmat, kqr, mom, mom_lo, mom_hi, part, part_other,
           load_sem, out_sem, xs_send, xs_recv, col_sem, z_send, z_recv, m_send, m_recv, s_sem):
    gx, gy, col = lax.axis_index("gx"), lax.axis_index("gy"), lax.axis_index("col")
    x_next, x_prev = lax.rem(gx + 1, nx), lax.rem(gx + nx - 1, nx)
    y_next, y_prev = lax.rem(gy + 1, ny), lax.rem(gy + ny - 1, ny)
    to_next, to_prev = (x_next, gy, col), (x_prev, gy, col)
    to_up, to_down = (gx, y_next, col), (gx, y_prev, col)
    to_col = (gx, gy, 1 - col)

    loads = [pltpu.make_async_copy(dens_hbm.at[pl.ds(p * 400, 400)], dens.at[pl.ds(p * 400, 400)],
                                   load_sem.at[p]) for p in range(P_HERE)]
    for c in loads:
        c.start()
    barrier = pltpu.get_barrier_semaphore()
    for d in (to_next, to_prev, to_up, to_down, to_col):
        pl.semaphore_signal(barrier, inc=1, device_id=d, device_id_type=MESH)

    def remote(src, dst, ss, rs, dev):
        return pltpu.make_async_remote_copy(src_ref=src, dst_ref=dst, send_sem=ss, recv_sem=rs,
                                            device_id=dev, device_id_type=MESH)

    x_copies = []
    for p in range(P_HERE):
        piece = pl.ds(p * 200, 200)
        x_copies.append((
            remote(send_hi.at[piece], recv_lo.at[piece], xs_send.at[0, p], xs_recv.at[0, p], to_next),
            remote(send_lo.at[piece], recv_hi.at[piece], xs_send.at[1, p], xs_recv.at[1, p], to_prev)))
    col_copy = remote(dens, other, col_sem.at[0], col_sem.at[1], to_col)
    z_copies = (remote(rim, rim_lo, z_send.at[0], z_recv.at[0], to_up),
                remote(rim, rim_hi, z_send.at[1], z_recv.at[1], to_down))
    m_copies = (remote(mom, mom_lo, m_send.at[0], m_recv.at[0], to_next),
                remote(mom, mom_hi, m_send.at[1], m_recv.at[1], to_prev))
    s_copy = remote(part, part_other, s_sem.at[0], s_sem.at[1], to_col)

    for p in range(P_HERE):
        loads[p].wait()
        for j in range(2):
            rows = pl.ds(p * 200 + j, QR, stride=2)
            send_lo[rows, :] = dens[pl.ds(p * 400 + j, QR, stride=WX), :]
            send_hi[rows, :] = dens[pl.ds(p * 400 + 2 + j, QR, stride=WX), :]
        if p == 0:
            pl.semaphore_wait(barrier, 5)
        if p < EARLY:
            for c in x_copies[p]:
                c.start()
    col_copy.start()

    lane = iota((8, WY), 1)

    def pack(g, _):
        tile = jnp.zeros((8, WY), jnp.float32)
        for k in range(PER):
            f = dens[pl.ds(pl.multiple_of(g * (8 * PER), 8) + 8 * k, 8), :]
            tile = jnp.where((lane >> 2) == k, pltpu.roll(f, (4 * k + 2) % WY, 1), tile)
        rim[pl.ds(pl.multiple_of(g * 8, 8), 8), :] = tile
        return 0

    lax.fori_loop(0, GROUPS, pack, 0)
    for c in z_copies:
        c.start()

    row, hot = iota((QR, HM), 0), iota((QR, HM), 1)
    row_t, hot_t = iota((HM, QR), 1), iota((HM, QR), 0)
    rr, cc = iota((QR, QR), 0), iota((QR, QR), 1)
    rq, cq = tenth(rr), tenth(cc)
    h_exp = dot(dot(one(tenth(row) == hot), herm[...]), one(tenth(row_t) == hot_t))
    l_exp = dot(dot(one(row - 10 * tenth(row) == hot), lag[...]), one(row_t - 10 * tenth(row_t) == hot_t))
    kqr[...] = time_step * (jnp.where(rr - 10 * rq == cc - 10 * cq, h_exp, 0.0) + jnp.where(rq == cq, l_exp, 0.0))

    def cells(tile, x):
        return tile[:, x * WY:(x + 1) * WY]

    u_pos = [-time_step * jnp.maximum(vel[0, x:x + 1, :], 0.0) for x in range(WX)]
    u_neg = [-time_step * jnp.minimum(vel[0, x:x + 1, :], 0.0) for x in range(WX)]

    mom[...] = jnp.zeros_like(mom)

    def own(p, _):
        c = [dens[pl.ds(p * 400 + x, QR, stride=WX), :] for x in range(WX)]
        block = jnp.concatenate(c, axis=1)
        rate = dot(kqr[...], block)
        mom[0:3, :] += dot(sw[p], block)
        for x in range(WX):
            value = cells(rate, x) + (1.5 * (u_pos[x] - u_neg[x])) * c[x]
            if x >= 1:
                value += (-2.0 * u_pos[x]) * c[x - 1]
            if x >= 2:
                value += (0.5 * u_pos[x]) * c[x - 2]
            if x < WX - 1:
                value += (2.0 * u_neg[x]) * c[x + 1]
            if x < WX - 2:
                value += (-0.5 * u_neg[x]) * c[x + 2]
            acc[pl.ds(p * 400 + x, QR, stride=WX), :] = value
        return 0

    lax.fori_loop(0, P_HERE, own, 0)
    for c in m_copies:
        c.start()
    for p in range(EARLY, P_HERE):
        for c in x_copies[p]:
            c.start()

    my0, other0 = col * P_HERE, (1 - col) * P_HERE
    r1, k1 = iota((PQ, 40), 0), iota((PQ, 40), 1)
    r1h, k1h = iota((PQ, HM), 0), iota((PQ, HM), 1)
    c2, j2 = iota((HM, 2 * PQ), 1), iota((HM, 2 * PQ), 0)
    near = c2 < PQ
    c2 = jnp.where(near, c2, c2 - PQ)
    real = c2 < 50
    p_hot = one(real & (j2 == jnp.where(near, my0, other0) + tenth(c2)))
    q_hot = one(real & (j2 == c2 - 10 * tenth(c2)))
    b_hot = one((r1h < 50) & (k1h == r1h - 10 * tenth(r1h)))
    a_hot = one((r1h < 50) & (k1h == my0 + tenth(r1h)))
    wmat[0:PQ, :] = time_step * dot(dot(a_hot, herm[...]), p_hot) * dot(b_hot, q_hot)
    for c in range(4):
        a_c = one((r1 < 50) & (k1 == 4 * (my0 + tenth(r1)) + c))
        b_c = one((r1 < 50) & (k1 == 4 * (r1 - 10 * tenth(r1)) + c))
        wmat[(c + 1) * PQ:(c + 2) * PQ, :] = time_step * (
            dot(dot(a_c, ff[...]), p_hot) * dot(dot(b_c, fs[...]), q_hot))
    xs[...] = jnp.zeros_like(xs)

    for c in z_copies:
        c.wait_recv()
    v = jnp.concatenate([vel[1], vel[1]], axis=0)
    v_pos = -time_step * jnp.maximum(v, 0.0)
    v_neg = -time_step * jnp.minimum(v, 0.0)
    k_0 = 1.0 + 1.5 * (v_pos - v_neg)
    k_m1, k_m2, k_p1, k_p2 = -2.0 * v_pos, 0.5 * v_pos, 2.0 * v_neg, -0.5 * v_neg
    low_wall = jnp.where(gy == 0, 0.0, 1.0).astype(jnp.float32)
    high_wall = jnp.where(gy == ny - 1, 0.0, 1.0).astype(jnp.float32)

    def normal(g, _):
        at = pl.ds(pl.multiple_of(g * 8, 8), 8)
        rims = jnp.where((lane & 3) < 2, rim_lo[at, :] * low_wall, rim_hi[at, :] * high_wall)
        for k in range(PER):
            here = pl.ds(pl.multiple_of(g * (8 * PER), 8) + 8 * k, 8)
            f = dens[here, :]
            h = pltpu.roll(rims, (2 * WY - 4 * k - 2) % WY, 1)
            m1 = pltpu.roll(jnp.where(lane == WY - 1, h, f), 1, 1)
            m2 = pltpu.roll(jnp.where(lane >= WY - 2, h, f), 2, 1)
            p1 = pltpu.roll(jnp.where(lane == 0, h, f), WY - 1, 1)
            p2 = pltpu.roll(jnp.where(lane < 2, h, f), WY - 2, 1)
            acc[here, :] += k_0 * f + k_m1 * m1 + k_m2 * m2 + k_p1 * p1 + k_p2 * p2
        return 0

    lax.fori_loop(0, GROUPS, normal, 0)

    col_copy.wait_recv()

    def couple(r, _):
        for x in range(WX):
            rows = pl.ds(r * WX + x, 50, stride=40)
            xs[0:50, x * WY:(x + 1) * WY] = dens[rows, :]
            xs[PQ:PQ + 50, x * WY:(x + 1) * WY] = other[rows, :]
        t = dot(wmat[...], xs[...])
        for x in range(WX):
            value = cells(t, x)[0:50]
            for c in range(4):
                value += shear[c, x:x + 1, :] * cells(t, x)[(c + 1) * PQ:(c + 1) * PQ + 50]
            acc[pl.ds(r * WX + x, 50, stride=40), :] += value
        return 0

    lax.fori_loop(0, HM, couple, 0)

    part[...] = jnp.zeros_like(part)

    def moments(p, _):
        block = jnp.concatenate([acc[pl.ds(p * 400 + x, QR, stride=WX), :] for x in range(WX)], axis=1)
        part[0:3, :] += dot(sw[p], block)
        return 0

    lax.fori_loop(0, P_HERE, moments, 0)
    for c in m_copies:
        c.wait_recv()

    def edges(lo2, lo1, hi0, hi1):
        return ((-2.0 * u_pos[0]) * lo1 + (0.5 * u_pos[0]) * lo2,
                (0.5 * u_pos[1]) * lo1,
                (-0.5 * u_neg[2]) * hi0,
                (2.0 * u_neg[3]) * hi0 + (-0.5 * u_neg[3]) * hi1)

    rims = edges(cells(mom_lo, 2), cells(mom_lo, 3), cells(mom_hi, 0), cells(mom_hi, 1))
    for x in range(WX):
        part[:, x * WY:(x + 1) * WY] += rims[x]
    s_copy.start()

    outs = []
    for p in range(P_HERE):
        for c in x_copies[p]:
            c.wait_recv()
        lo2, lo1 = (recv_lo[pl.ds(p * 200 + j, QR, stride=2), :] for j in range(2))
        hi0, hi1 = (recv_hi[pl.ds(p * 200 + j, QR, stride=2), :] for j in range(2))
        add = edges(lo2, lo1, hi0, hi1)
        for x in range(WX):
            acc[pl.ds(p * 400 + x, QR, stride=WX), :] += add[x]
        out = pltpu.make_async_copy(acc.at[pl.ds(p * 400, 400)], out_hbm.at[pl.ds(p * 400, 400)], out_sem.at[p])
        out.start()
        outs.append(out)
    s_copy.wait_recv()
    total = part[...] + part_other[...]
    for x in range(WX):
        stress_out[:, x, :] = cells(total, x)[0:3]
    for pair in x_copies + [z_copies, m_copies, (col_copy, s_copy)]:
        for c in pair:
            c.wait_send()
    for out in outs:
        out.wait()


def body(nx, ny, density, velocity, shear_rates, hermite_matrix, laguerre_matrix, flow_first,
         flow_second, stress_weights):
    assert density.shape == (P_HERE, HM, HM, WX, WY)
    f32 = jnp.float32
    vmem = pl.BlockSpec(memory_space=pltpu.VMEM)
    hbm = pl.BlockSpec(memory_space=pl.ANY)
    dma = pltpu.SemaphoreType.DMA
    advanced, stress = pl.pallas_call(
        functools.partial(kernel, nx, ny),
        out_shape=(jax.ShapeDtypeStruct((ROWS, WY), f32), jax.ShapeDtypeStruct((3, WX, WY), f32)),
        in_specs=[hbm] + [vmem] * 7,
        out_specs=(hbm, vmem),
        scratch_shapes=[
            pltpu.VMEM((ROWS, WY), f32), pltpu.VMEM((ROWS, WY), f32), pltpu.VMEM((ROWS, WY), f32),
            pltpu.VMEM((ROWS // 2, WY), f32), pltpu.VMEM((ROWS // 2, WY), f32),
            pltpu.VMEM((ROWS // 2, WY), f32), pltpu.VMEM((ROWS // 2, WY), f32),
            pltpu.VMEM((8 * GROUPS, WY), f32), pltpu.VMEM((8 * GROUPS, WY), f32), pltpu.VMEM((8 * GROUPS, WY), f32),
            pltpu.VMEM((2 * PQ, WX * WY), f32), pltpu.VMEM((5 * PQ, 2 * PQ), f32), pltpu.VMEM((QR, QR), f32),
            pltpu.VMEM((8, WX * WY), f32), pltpu.VMEM((8, WX * WY), f32), pltpu.VMEM((8, WX * WY), f32),
            pltpu.VMEM((8, WX * WY), f32), pltpu.VMEM((8, WX * WY), f32),
            dma((P_HERE,)), dma((P_HERE,)), dma((2, P_HERE)), dma((2, P_HERE)), dma((2,)),
            dma((2,)), dma((2,)), dma((2,)), dma((2,)), dma((2,)),
        ],
        compiler_params=pltpu.CompilerParams(collective_id=0, has_side_effects=True,
                                             vmem_limit_bytes=32 * 1024 * 1024),
        cost_estimate=pl.CostEstimate(flops=600_000_000, bytes_accessed=3_000_000, transcendentals=0),
    )(
        density.reshape(ROWS, WY), velocity, shear_rates, hermite_matrix, laguerre_matrix,
        flow_first.transpose(1, 0, 2).reshape(4 * HM, HM), flow_second.transpose(1, 0, 2).reshape(4 * HM, HM),
        stress_weights.reshape(3, P_HERE, QR).transpose(1, 0, 2),
    )
    return advanced.reshape(density.shape), stress


def solution(mesh):
    in_specs = (
        P("col", None, None, "gx", "gy"),
        P(None, "gx", "gy"),
        P(None, "gx", "gy"),
        P(),
        P(),
        P(),
        P(),
        P(None, "col", None, None),
    )
    out_specs = (P("col", None, None, "gx", "gy"), P(None, "gx", "gy"))
    one_device = functools.partial(body, mesh.shape["gx"], mesh.shape["gy"])
    return jax.shard_map(one_device, mesh=mesh, in_specs=in_specs, out_specs=out_specs, check_vma=False)
```

```python
import functools

import jax
import jax.numpy as jnp
from jax import lax
from jax.experimental import pallas as pl
from jax.experimental.pallas import tpu as pltpu
from jax.sharding import PartitionSpec as P

time_step = 0.1
highest = lax.Precision.HIGHEST
MESH = pl.DeviceIdType.MESH

P_HERE = 5
HM = 10
QR = 100
WX = 4
WY = 128
ROWS = P_HERE * QR * WX
PQ = 56
WR = 288
GROUPS, PER = 10, 25
EARLY = 4
LAST = P_HERE - 1


def dot(a, b):
    return jnp.dot(a, b, precision=highest, preferred_element_type=jnp.float32)


def tenth(i):
    return lax.shift_right_logical(i * 205, 11)


def iota(shape, axis):
    return lax.broadcasted_iota(jnp.int32, shape, axis)


def one(cond):
    return jnp.where(cond, 1.0, 0.0).astype(jnp.float32)


def halves(a):
    hi = a.astype(jnp.bfloat16)
    return hi, (a - hi.astype(jnp.float32)).astype(jnp.bfloat16)


def dot3(a_hi, a_lo, b):
    b_hi, b_lo = halves(b)
    mul = functools.partial(jnp.dot, preferred_element_type=jnp.float32)
    return mul(a_hi, b_hi) + (mul(a_hi, b_lo) + mul(a_lo, b_hi))


def cells(tile, x):
    return tile[:, x * WY:(x + 1) * WY]


def speeds(vel):
    u_pos = [-time_step * jnp.maximum(vel[0, x:x + 1, :], 0.0) for x in range(WX)]
    u_neg = [-time_step * jnp.minimum(vel[0, x:x + 1, :], 0.0) for x in range(WX)]
    return u_pos, u_neg


def edges(u_pos, u_neg, lo2, lo1, hi0, hi1):
    return ((-2.0 * u_pos[0]) * lo1 + (0.5 * u_pos[0]) * lo2,
            (0.5 * u_pos[1]) * lo1,
            (-0.5 * u_neg[2]) * hi0,
            (2.0 * u_neg[3]) * hi0 + (-0.5 * u_neg[3]) * hi1)


def rim_terms(vel, recv_lo, recv_hi, p):
    lo2, lo1 = (recv_lo[pl.ds(p * 200 + j, QR, stride=2), :] for j in range(2))
    hi0, hi1 = (recv_hi[pl.ds(p * 200 + j, QR, stride=2), :] for j in range(2))
    return edges(*speeds(vel), lo2, lo1, hi0, hi1)


def kernel(nx, ny, dens_hbm, vel_hbm, shear_hbm, herm_hbm, lag_hbm, ff_hbm, fs_hbm, sw_hbm,
           acc, recv_lo, recv_hi, part, part_other,
           dens, other, vel, shear, herm, lag, ff, fs, sw_in, sw_rows, sw,
           send_lo, send_hi, rim, rim_lo, rim_hi,
           xs, w_hi, w_lo, kqr_hi, kqr_lo, mom, mom_lo, mom_hi,
           load_sem, in_sem, xs_send, xs_recv, col_sem, z_send, z_recv, m_send, m_recv, s_sem):
    gx, gy, col = lax.axis_index("gx"), lax.axis_index("gy"), lax.axis_index("col")
    x_next, x_prev = lax.rem(gx + 1, nx), lax.rem(gx + nx - 1, nx)
    y_next, y_prev = lax.rem(gy + 1, ny), lax.rem(gy + ny - 1, ny)
    to_next, to_prev = (x_next, gy, col), (x_prev, gy, col)
    to_up, to_down = (gx, y_next, col), (gx, y_prev, col)
    to_col = (gx, gy, 1 - col)

    loads = [pltpu.make_async_copy(dens_hbm.at[pl.ds(p * 400, 400)], dens.at[pl.ds(p * 400, 400)],
                                   load_sem.at[p]) for p in range(P_HERE)]
    smalls = [pltpu.make_async_copy(src, dst, in_sem.at[i]) for i, (src, dst) in enumerate((
        (vel_hbm, vel), (herm_hbm, herm), (lag_hbm, lag), (sw_hbm, sw_in),
        (ff_hbm, ff), (fs_hbm, fs), (shear_hbm, shear)))]
    for c in loads + smalls:
        c.start()
    barrier = pltpu.get_barrier_semaphore()
    for d in (to_next, to_prev, to_up, to_down, to_col):
        pl.semaphore_signal(barrier, inc=1, device_id=d, device_id_type=MESH)

    def remote(src, dst, ss, rs, dev):
        return pltpu.make_async_remote_copy(src_ref=src, dst_ref=dst, send_sem=ss, recv_sem=rs,
                                            device_id=dev, device_id_type=MESH)

    x_copies = []
    for p in range(P_HERE):
        piece = pl.ds(p * 200, 200)
        x_copies.append((
            remote(send_hi.at[piece], recv_lo.at[piece], xs_send.at[0, p], xs_recv.at[0, p], to_next),
            remote(send_lo.at[piece], recv_hi.at[piece], xs_send.at[1, p], xs_recv.at[1, p], to_prev)))
    col_copy = remote(dens, other, col_sem.at[0], col_sem.at[1], to_col)
    z_copies = (remote(rim, rim_lo, z_send.at[0], z_recv.at[0], to_up),
                remote(rim, rim_hi, z_send.at[1], z_recv.at[1], to_down))
    m_copies = (remote(mom, mom_lo, m_send.at[0], m_recv.at[0], to_next),
                remote(mom, mom_hi, m_send.at[1], m_recv.at[1], to_prev))
    s_copy = remote(part, part_other, s_sem.at[0], s_sem.at[1], to_col)

    for p in range(P_HERE):
        loads[p].wait()
        for j in range(2):
            rows = pl.ds(p * 200 + j, QR, stride=2)
            send_lo[rows, :] = dens[pl.ds(p * 400 + j, QR, stride=WX), :]
            send_hi[rows, :] = dens[pl.ds(p * 400 + 2 + j, QR, stride=WX), :]
        if p == 0:
            pl.semaphore_wait(barrier, 5)
        if p < EARLY:
            for c in x_copies[p]:
                c.start()
    col_copy.start()

    lane = iota((8, WY), 1)

    def pack(g, _):
        tile = jnp.zeros((8, WY), jnp.float32)
        for k in range(PER):
            f = dens[pl.ds(pl.multiple_of(g * (8 * PER), 8) + 8 * k, 8), :]
            tile = jnp.where((lane >> 2) == k, pltpu.roll(f, (4 * k + 2) % WY, 1), tile)
        rim[pl.ds(pl.multiple_of(g * 8, 8), 8), :] = tile
        return 0

    lax.fori_loop(0, GROUPS, pack, 0)
    for c in z_copies:
        c.start()

    for c in smalls:
        c.wait()
    sw_rows[...] = jnp.zeros_like(sw_rows)
    for p in range(P_HERE):
        for q in range(HM):
            at = (p * HM + q) * 8
            sw_rows[at:at + 3, :] = sw_in[p, q]
    lane_qr = iota((8, QR), 1)
    q_of, r_hot = tenth(lane_qr), iota((HM, QR), 1)
    spread = dot(sw_rows[...], one(r_hot - 10 * tenth(r_hot) == iota((HM, QR), 0)))
    for p in range(P_HERE):
        sw[p] = sum(jnp.where(q_of == q, spread[(p * HM + q) * 8:(p * HM + q) * 8 + 8], 0.0) for q in range(HM))

    row, hot = iota((QR, HM), 0), iota((QR, HM), 1)
    row_t, hot_t = iota((HM, QR), 1), iota((HM, QR), 0)
    rr, cc = iota((QR, QR), 0), iota((QR, QR), 1)
    rq, cq = tenth(rr), tenth(cc)
    h_exp = dot(dot(one(tenth(row) == hot), herm[...]), one(tenth(row_t) == hot_t))
    l_exp = dot(dot(one(row - 10 * tenth(row) == hot), lag[...]), one(row_t - 10 * tenth(row_t) == hot_t))
    kqr_hi[...], kqr_lo[...] = halves(time_step * (jnp.where(rr - 10 * rq == cc - 10 * cq, h_exp, 0.0) + jnp.where(rq == cq, l_exp, 0.0)))

    u_pos, u_neg = speeds(vel)

    mom[...] = jnp.zeros_like(mom)

    def own(p, _):
        c = [dens[pl.ds(p * 400 + x, QR, stride=WX), :] for x in range(WX)]
        block = jnp.concatenate(c, axis=1)
        rate = dot3(kqr_hi[...], kqr_lo[...], block)
        mom[...] += dot(sw[p], block)
        for x in range(WX):
            value = cells(rate, x) + (1.5 * (u_pos[x] - u_neg[x])) * c[x]
            if x >= 1:
                value += (-2.0 * u_pos[x]) * c[x - 1]
            if x >= 2:
                value += (0.5 * u_pos[x]) * c[x - 2]
            if x < WX - 1:
                value += (2.0 * u_neg[x]) * c[x + 1]
            if x < WX - 2:
                value += (-0.5 * u_neg[x]) * c[x + 2]
            acc[pl.ds(p * 400 + x, QR, stride=WX), :] = value
        return 0

    lax.fori_loop(0, P_HERE, own, 0)
    for c in m_copies:
        c.start()
    for p in range(EARLY, P_HERE):
        for c in x_copies[p]:
            c.start()

    my0, other0 = col * P_HERE, (1 - col) * P_HERE
    r1, k1 = iota((WR, 50), 0), iota((WR, 50), 1)
    comp = sum(jnp.where(r1 >= PQ * c, 1, 0) for c in range(1, 5))
    r1 = jnp.where(r1 < 5 * PQ, r1 - PQ * comp, PQ)
    flow, a_of = comp < 4, tenth(r1)
    b_of = r1 - 10 * a_of
    a_hot = one((r1 < 50) & (k1 == jnp.where(flow, 4 * (my0 + a_of) + comp, 40 + my0 + a_of)))
    b_hot = one((r1 < 50) & (k1 == jnp.where(flow, 4 * b_of + comp, 40 + b_of)))
    c2, j2 = iota((HM, 2 * PQ), 1), iota((HM, 2 * PQ), 0)
    near = c2 < PQ
    c2 = jnp.where(near, c2, c2 - PQ)
    real = c2 < 50
    p_hot = one(real & (j2 == jnp.where(near, my0, other0) + tenth(c2)))
    q_hot = one(real & (j2 == c2 - 10 * tenth(c2)))
    eye = one(iota((HM, HM), 0) == iota((HM, HM), 1))
    first = dot(dot(a_hot, jnp.concatenate([ff[...], herm[...]], axis=0)), p_hot)
    second = dot(dot(b_hot, jnp.concatenate([fs[...], eye], axis=0)), q_hot)
    w_hi[...], w_lo[...] = halves(time_step * first * second)
    xs[...] = jnp.zeros_like(xs)

    for c in z_copies:
        c.wait_recv()
    v = jnp.concatenate([vel[1], vel[1]], axis=0)
    v_pos = -time_step * jnp.maximum(v, 0.0)
    v_neg = -time_step * jnp.minimum(v, 0.0)
    k_0 = 1.0 + 1.5 * (v_pos - v_neg)
    k_m1, k_m2, k_p1, k_p2 = -2.0 * v_pos, 0.5 * v_pos, 2.0 * v_neg, -0.5 * v_neg
    low_wall = jnp.where(gy == 0, 0.0, 1.0).astype(jnp.float32)
    high_wall = jnp.where(gy == ny - 1, 0.0, 1.0).astype(jnp.float32)

    def normal(g, _):
        at = pl.ds(pl.multiple_of(g * 8, 8), 8)
        rims = jnp.where((lane & 3) < 2, rim_lo[at, :] * low_wall, rim_hi[at, :] * high_wall)
        for k in range(PER):
            here = pl.ds(pl.multiple_of(g * (8 * PER), 8) + 8 * k, 8)
            f = dens[here, :]
            h = pltpu.roll(rims, (2 * WY - 4 * k - 2) % WY, 1)
            m1 = pltpu.roll(jnp.where(lane == WY - 1, h, f), 1, 1)
            m2 = pltpu.roll(jnp.where(lane >= WY - 2, h, f), 2, 1)
            p1 = pltpu.roll(jnp.where(lane == 0, h, f), WY - 1, 1)
            p2 = pltpu.roll(jnp.where(lane < 2, h, f), WY - 2, 1)
            acc[here, :] += k_0 * f + k_m1 * m1 + k_m2 * m2 + k_p1 * p1 + k_p2 * p2
        return 0

    lax.fori_loop(0, GROUPS, normal, 0)

    col_copy.wait_recv()

    def couple(r, _):
        for x in range(WX):
            rows = pl.ds(r * WX + x, 50, stride=40)
            xs[0:50, x * WY:(x + 1) * WY] = dens[rows, :]
            xs[PQ:PQ + 50, x * WY:(x + 1) * WY] = other[rows, :]
        t = dot3(w_hi[...], w_lo[...], xs[...])
        for x in range(WX):
            value = cells(t, x)[4 * PQ:4 * PQ + 50]
            for c in range(4):
                value += shear[c, x:x + 1, :] * cells(t, x)[c * PQ:c * PQ + 50]
            acc[pl.ds(r * WX + x, 50, stride=40), :] += value
        return 0

    lax.fori_loop(0, HM, couple, 0)

    part[...] = jnp.zeros_like(part)

    def moments(p, _):
        block = jnp.concatenate([acc[pl.ds(p * 400 + x, QR, stride=WX), :] for x in range(WX)], axis=1)
        part[...] += dot(sw[p], block)
        return 0

    lax.fori_loop(0, P_HERE, moments, 0)
    for c in m_copies:
        c.wait_recv()

    rims = edges(u_pos, u_neg, cells(mom_lo, 2), cells(mom_lo, 3), cells(mom_hi, 0), cells(mom_hi, 1))
    for x in range(WX):
        part[:, x * WY:(x + 1) * WY] += rims[x]
    s_copy.start()

    for p in range(P_HERE):
        for c in x_copies[p]:
            c.wait_recv()
        if p < LAST:
            add = rim_terms(vel, recv_lo, recv_hi, p)
            for x in range(WX):
                acc[pl.ds(p * 400 + x, QR, stride=WX), :] += add[x]
    s_copy.wait_recv()
    for pair in x_copies + [z_copies, m_copies, (col_copy, s_copy)]:
        for c in pair:
            c.wait_send()


def finish(acc, recv_lo, recv_hi, part, part_other, vel, out_hbm, stress_out, last, sem):
    outs = [pltpu.make_async_copy(acc.at[pl.ds(p * 400, 400)], out_hbm.at[pl.ds(p * 400, 400)], sem.at[p])
            for p in range(LAST)]
    outs.append(pltpu.make_async_copy(last, out_hbm.at[pl.ds(LAST * 400, 400)], sem.at[LAST]))
    for c in outs[:LAST]:
        c.start()
    add = rim_terms(vel, recv_lo, recv_hi, LAST)
    for x in range(WX):
        last[pl.ds(x, QR, stride=WX), :] = acc[pl.ds(LAST * 400 + x, QR, stride=WX), :] + add[x]
    outs[LAST].start()
    total = part[...] + part_other[...]
    for x in range(WX):
        stress_out[:, x, :] = cells(total, x)[0:3]
    for c in outs:
        c.wait()


def body(nx, ny, density, velocity, shear_rates, hermite_matrix, laguerre_matrix, flow_first,
         flow_second, stress_weights):
    assert density.shape == (P_HERE, HM, HM, WX, WY)
    f32, bf16 = jnp.float32, jnp.bfloat16
    vmem = pl.BlockSpec(memory_space=pltpu.VMEM)
    hbm = pl.BlockSpec(memory_space=pltpu.HBM)
    dma = pltpu.SemaphoreType.DMA
    whole, half = (ROWS, WY), (ROWS // 2, WY)
    rims, sums = (8 * GROUPS, WY), (8, WX * WY)
    flows = (4 * HM, HM)
    acc, recv_lo, recv_hi, part, part_other = pl.pallas_call(
        functools.partial(kernel, nx, ny),
        out_shape=[jax.ShapeDtypeStruct(s, f32) for s in (whole, half, half, sums, sums)],
        in_specs=[hbm] * 8,
        out_specs=[vmem] * 5,
        scratch_shapes=[
            pltpu.VMEM(whole, f32), pltpu.VMEM(whole, f32),
            pltpu.VMEM((2, WX, WY), f32), pltpu.VMEM((4, WX, WY), f32),
            pltpu.VMEM((HM, HM), f32), pltpu.VMEM((HM, HM), f32),
            pltpu.VMEM(flows, f32), pltpu.VMEM(flows, f32),
            pltpu.VMEM((P_HERE, HM, 3, HM), f32), pltpu.VMEM((P_HERE * HM * 8, HM), f32),
            pltpu.VMEM((P_HERE, 8, QR), f32),
            pltpu.VMEM(half, f32), pltpu.VMEM(half, f32),
            pltpu.VMEM(rims, f32), pltpu.VMEM(rims, f32), pltpu.VMEM(rims, f32),
            pltpu.VMEM((2 * PQ, WX * WY), f32), pltpu.VMEM((WR, 2 * PQ), bf16), pltpu.VMEM((WR, 2 * PQ), bf16),
            pltpu.VMEM((QR, QR), bf16), pltpu.VMEM((QR, QR), bf16),
            pltpu.VMEM(sums, f32), pltpu.VMEM(sums, f32), pltpu.VMEM(sums, f32),
            dma((P_HERE,)), dma((7,)), dma((2, P_HERE)), dma((2, P_HERE)), dma((2,)),
            dma((2,)), dma((2,)), dma((2,)), dma((2,)), dma((2,)),
        ],
        compiler_params=pltpu.CompilerParams(collective_id=0, has_side_effects=True,
                                             vmem_limit_bytes=52700 * 1024),
        cost_estimate=pl.CostEstimate(flops=600_000_000, bytes_accessed=3_000_000, transcendentals=0),
    )(
        density.reshape(whole), velocity, shear_rates, hermite_matrix, laguerre_matrix,
        flow_first.transpose(1, 0, 2).reshape(flows), flow_second.transpose(1, 0, 2).reshape(flows),
        stress_weights.transpose(1, 2, 0, 3),
    )
    advanced, stress = pl.pallas_call(
        finish,
        out_shape=(jax.ShapeDtypeStruct(whole, f32), jax.ShapeDtypeStruct((3, WX, WY), f32)),
        in_specs=[vmem] * 6,
        out_specs=(hbm, vmem),
        scratch_shapes=[pltpu.VMEM((QR * WX, WY), f32), dma((P_HERE,))],
        cost_estimate=pl.CostEstimate(flops=1_000_000, bytes_accessed=2_000_000, transcendentals=0),
    )(acc, recv_lo, recv_hi, part, part_other, velocity)
    return advanced.reshape(density.shape), stress


def solution(mesh):
    in_specs = (
        P("col", None, None, "gx", "gy"),
        P(None, "gx", "gy"),
        P(None, "gx", "gy"),
        P(),
        P(),
        P(),
        P(),
        P(None, "col", None, None),
    )
    out_specs = (P("col", None, None, "gx", "gy"), P(None, "gx", "gy"))
    one_device = functools.partial(body, mesh.shape["gx"], mesh.shape["gy"])
    return jax.shard_map(one_device, mesh=mesh, in_specs=in_specs, out_specs=out_specs, check_vma=False)
```

```python
import functools

import jax
import jax.numpy as jnp
from jax import lax
from jax.experimental import pallas as pl
from jax.experimental.pallas import tpu as pltpu
from jax.sharding import PartitionSpec as P

time_step = 0.1
highest = lax.Precision.HIGHEST
MESH = pl.DeviceIdType.MESH

P_HERE = 5
HM = 10
QR = 100
WX = 4
WY = 128
ROWS = P_HERE * QR * WX
PQ = 56
WR = 288
GROUPS, PER = 10, 25
EARLY = 4
LAST = P_HERE - 1


def dot(a, b):
    return jnp.dot(a, b, precision=highest, preferred_element_type=jnp.float32)


def tenth(i):
    return lax.shift_right_logical(i * 205, 11)


def iota(shape, axis):
    return lax.broadcasted_iota(jnp.int32, shape, axis)


def one(cond):
    return jnp.where(cond, 1.0, 0.0).astype(jnp.float32)


def halves(a):
    hi = a.astype(jnp.bfloat16)
    return hi, (a - hi.astype(jnp.float32)).astype(jnp.bfloat16)


def dot3(a_hi, a_lo, b):
    b_hi, b_lo = halves(b)
    mul = functools.partial(jnp.dot, preferred_element_type=jnp.float32)
    return mul(a_hi, b_hi) + (mul(a_hi, b_lo) + mul(a_lo, b_hi))


def cells(tile, x):
    return tile[:, x * WY:(x + 1) * WY]


def speeds(vel):
    u_pos = [-time_step * jnp.maximum(vel[0, x:x + 1, :], 0.0) for x in range(WX)]
    u_neg = [-time_step * jnp.minimum(vel[0, x:x + 1, :], 0.0) for x in range(WX)]
    return u_pos, u_neg


def edges(u_pos, u_neg, lo2, lo1, hi0, hi1):
    return ((-2.0 * u_pos[0]) * lo1 + (0.5 * u_pos[0]) * lo2,
            (0.5 * u_pos[1]) * lo1,
            (-0.5 * u_neg[2]) * hi0,
            (2.0 * u_neg[3]) * hi0 + (-0.5 * u_neg[3]) * hi1)


def rim_terms(vel, recv_lo, recv_hi, p):
    lo2, lo1 = (recv_lo[pl.ds(p * 200 + j, QR, stride=2), :] for j in range(2))
    hi0, hi1 = (recv_hi[pl.ds(p * 200 + j, QR, stride=2), :] for j in range(2))
    return edges(*speeds(vel), lo2, lo1, hi0, hi1)


def kernel(nx, ny, dens_hbm, vel_hbm, shear_hbm, herm_hbm, lag_hbm, ff_hbm, fs_hbm, sw_hbm,
           out_hbm, stress_hbm,
           acc, recv_lo, recv_hi, part, part_other, stress, dens, other, vel, shear, herm, lag, ff, fs, sw_in, sw_rows, sw,
           send_lo, send_hi, rim, rim_lo, rim_hi,
           xs, w_hi, w_lo, kqr_hi, kqr_lo, mom, mom_lo, mom_hi,
           load_sem, in_sem, out_sem, xs_send, xs_recv, col_sem, z_send, z_recv, m_send, m_recv, s_sem):
    gx, gy, col = lax.axis_index("gx"), lax.axis_index("gy"), lax.axis_index("col")
    x_next, x_prev = lax.rem(gx + 1, nx), lax.rem(gx + nx - 1, nx)
    y_next, y_prev = lax.rem(gy + 1, ny), lax.rem(gy + ny - 1, ny)
    to_next, to_prev = (x_next, gy, col), (x_prev, gy, col)
    to_up, to_down = (gx, y_next, col), (gx, y_prev, col)
    to_col = (gx, gy, 1 - col)

    loads = [pltpu.make_async_copy(dens_hbm.at[pl.ds(p * 400, 400)], dens.at[pl.ds(p * 400, 400)],
                                   load_sem.at[p]) for p in range(P_HERE)]
    smalls = [pltpu.make_async_copy(src, dst, in_sem.at[i]) for i, (src, dst) in enumerate((
        (vel_hbm, vel), (herm_hbm, herm), (lag_hbm, lag), (sw_hbm, sw_in),
        (ff_hbm, ff), (fs_hbm, fs), (shear_hbm, shear)))]
    for c in loads + smalls:
        c.start()
    barrier = pltpu.get_barrier_semaphore()
    for d in (to_next, to_prev, to_up, to_down, to_col):
        pl.semaphore_signal(barrier, inc=1, device_id=d, device_id_type=MESH)

    def remote(src, dst, ss, rs, dev):
        return pltpu.make_async_remote_copy(src_ref=src, dst_ref=dst, send_sem=ss, recv_sem=rs,
                                            device_id=dev, device_id_type=MESH)

    x_copies = []
    for p in range(P_HERE):
        piece = pl.ds(p * 200, 200)
        x_copies.append((
            remote(send_hi.at[piece], recv_lo.at[piece], xs_send.at[0, p], xs_recv.at[0, p], to_next),
            remote(send_lo.at[piece], recv_hi.at[piece], xs_send.at[1, p], xs_recv.at[1, p], to_prev)))
    col_copy = remote(dens, other, col_sem.at[0], col_sem.at[1], to_col)
    z_copies = (remote(rim, rim_lo, z_send.at[0], z_recv.at[0], to_up),
                remote(rim, rim_hi, z_send.at[1], z_recv.at[1], to_down))
    m_copies = (remote(mom, mom_lo, m_send.at[0], m_recv.at[0], to_next),
                remote(mom, mom_hi, m_send.at[1], m_recv.at[1], to_prev))
    s_copy = remote(part, part_other, s_sem.at[0], s_sem.at[1], to_col)

    for p in range(P_HERE):
        loads[p].wait()
        for j in range(2):
            rows = pl.ds(p * 200 + j, QR, stride=2)
            send_lo[rows, :] = dens[pl.ds(p * 400 + j, QR, stride=WX), :]
            send_hi[rows, :] = dens[pl.ds(p * 400 + 2 + j, QR, stride=WX), :]
        if p == 0:
            pl.semaphore_wait(barrier, 5)
        if p < EARLY:
            for c in x_copies[p]:
                c.start()
    col_copy.start()

    lane = iota((8, WY), 1)

    def pack(g, _):
        tile = jnp.zeros((8, WY), jnp.float32)
        for k in range(PER):
            f = dens[pl.ds(pl.multiple_of(g * (8 * PER), 8) + 8 * k, 8), :]
            tile = jnp.where((lane >> 2) == k, pltpu.roll(f, (4 * k + 2) % WY, 1), tile)
        rim[pl.ds(pl.multiple_of(g * 8, 8), 8), :] = tile
        return 0

    lax.fori_loop(0, GROUPS, pack, 0)
    for c in z_copies:
        c.start()

    for c in smalls:
        c.wait()
    sw_rows[...] = jnp.zeros_like(sw_rows)
    for p in range(P_HERE):
        for q in range(HM):
            at = (p * HM + q) * 8
            sw_rows[at:at + 3, :] = sw_in[p, q]
    lane_qr = iota((8, QR), 1)
    q_of, r_hot = tenth(lane_qr), iota((HM, QR), 1)
    spread = dot(sw_rows[...], one(r_hot - 10 * tenth(r_hot) == iota((HM, QR), 0)))
    for p in range(P_HERE):
        sw[p] = sum(jnp.where(q_of == q, spread[(p * HM + q) * 8:(p * HM + q) * 8 + 8], 0.0) for q in range(HM))

    row, hot = iota((QR, HM), 0), iota((QR, HM), 1)
    row_t, hot_t = iota((HM, QR), 1), iota((HM, QR), 0)
    rr, cc = iota((QR, QR), 0), iota((QR, QR), 1)
    rq, cq = tenth(rr), tenth(cc)
    h_exp = dot(dot(one(tenth(row) == hot), herm[...]), one(tenth(row_t) == hot_t))
    l_exp = dot(dot(one(row - 10 * tenth(row) == hot), lag[...]), one(row_t - 10 * tenth(row_t) == hot_t))
    kqr_hi[...], kqr_lo[...] = halves(time_step * (jnp.where(rr - 10 * rq == cc - 10 * cq, h_exp, 0.0) + jnp.where(rq == cq, l_exp, 0.0)))

    u_pos, u_neg = speeds(vel)

    mom[...] = jnp.zeros_like(mom)

    def own(p, _):
        c = [dens[pl.ds(p * 400 + x, QR, stride=WX), :] for x in range(WX)]
        block = jnp.concatenate(c, axis=1)
        rate = dot3(kqr_hi[...], kqr_lo[...], block)
        mom[...] += dot(sw[p], block)
        for x in range(WX):
            value = cells(rate, x) + (1.5 * (u_pos[x] - u_neg[x])) * c[x]
            if x >= 1:
                value += (-2.0 * u_pos[x]) * c[x - 1]
            if x >= 2:
                value += (0.5 * u_pos[x]) * c[x - 2]
            if x < WX - 1:
                value += (2.0 * u_neg[x]) * c[x + 1]
            if x < WX - 2:
                value += (-0.5 * u_neg[x]) * c[x + 2]
            acc[pl.ds(p * 400 + x, QR, stride=WX), :] = value
        return 0

    lax.fori_loop(0, P_HERE, own, 0)
    for c in m_copies:
        c.start()
    for p in range(EARLY, P_HERE):
        for c in x_copies[p]:
            c.start()

    my0, other0 = col * P_HERE, (1 - col) * P_HERE
    r1, k1 = iota((WR, 50), 0), iota((WR, 50), 1)
    comp = sum(jnp.where(r1 >= PQ * c, 1, 0) for c in range(1, 5))
    r1 = jnp.where(r1 < 5 * PQ, r1 - PQ * comp, PQ)
    flow, a_of = comp < 4, tenth(r1)
    b_of = r1 - 10 * a_of
    a_hot = one((r1 < 50) & (k1 == jnp.where(flow, 4 * (my0 + a_of) + comp, 40 + my0 + a_of)))
    b_hot = one((r1 < 50) & (k1 == jnp.where(flow, 4 * b_of + comp, 40 + b_of)))
    c2, j2 = iota((HM, 2 * PQ), 1), iota((HM, 2 * PQ), 0)
    near = c2 < PQ
    c2 = jnp.where(near, c2, c2 - PQ)
    real = c2 < 50
    p_hot = one(real & (j2 == jnp.where(near, my0, other0) + tenth(c2)))
    q_hot = one(real & (j2 == c2 - 10 * tenth(c2)))
    eye = one(iota((HM, HM), 0) == iota((HM, HM), 1))
    first = dot(dot(a_hot, jnp.concatenate([ff[...], herm[...]], axis=0)), p_hot)
    second = dot(dot(b_hot, jnp.concatenate([fs[...], eye], axis=0)), q_hot)
    w_hi[...], w_lo[...] = halves(time_step * first * second)
    xs[...] = jnp.zeros_like(xs)

    for c in z_copies:
        c.wait_recv()
    v = jnp.concatenate([vel[1], vel[1]], axis=0)
    v_pos = -time_step * jnp.maximum(v, 0.0)
    v_neg = -time_step * jnp.minimum(v, 0.0)
    k_0 = 1.0 + 1.5 * (v_pos - v_neg)
    k_m1, k_m2, k_p1, k_p2 = -2.0 * v_pos, 0.5 * v_pos, 2.0 * v_neg, -0.5 * v_neg
    low_wall = jnp.where(gy == 0, 0.0, 1.0).astype(jnp.float32)
    high_wall = jnp.where(gy == ny - 1, 0.0, 1.0).astype(jnp.float32)

    def normal(g, _):
        at = pl.ds(pl.multiple_of(g * 8, 8), 8)
        rims = jnp.where((lane & 3) < 2, rim_lo[at, :] * low_wall, rim_hi[at, :] * high_wall)
        for k in range(PER):
            here = pl.ds(pl.multiple_of(g * (8 * PER), 8) + 8 * k, 8)
            f = dens[here, :]
            h = pltpu.roll(rims, (2 * WY - 4 * k - 2) % WY, 1)
            m1 = pltpu.roll(jnp.where(lane == WY - 1, h, f), 1, 1)
            m2 = pltpu.roll(jnp.where(lane >= WY - 2, h, f), 2, 1)
            p1 = pltpu.roll(jnp.where(lane == 0, h, f), WY - 1, 1)
            p2 = pltpu.roll(jnp.where(lane < 2, h, f), WY - 2, 1)
            acc[here, :] += k_0 * f + k_m1 * m1 + k_m2 * m2 + k_p1 * p1 + k_p2 * p2
        return 0

    lax.fori_loop(0, GROUPS, normal, 0)

    col_copy.wait_recv()

    def couple(r, _):
        for x in range(WX):
            rows = pl.ds(r * WX + x, 50, stride=40)
            xs[0:50, x * WY:(x + 1) * WY] = dens[rows, :]
            xs[PQ:PQ + 50, x * WY:(x + 1) * WY] = other[rows, :]
        t = dot3(w_hi[...], w_lo[...], xs[...])
        for x in range(WX):
            value = cells(t, x)[4 * PQ:4 * PQ + 50]
            for c in range(4):
                value += shear[c, x:x + 1, :] * cells(t, x)[c * PQ:c * PQ + 50]
            acc[pl.ds(r * WX + x, 50, stride=40), :] += value
        return 0

    lax.fori_loop(0, HM, couple, 0)

    part[...] = jnp.zeros_like(part)

    def moments(p, _):
        block = jnp.concatenate([acc[pl.ds(p * 400 + x, QR, stride=WX), :] for x in range(WX)], axis=1)
        part[...] += dot(sw[p], block)
        return 0

    lax.fori_loop(0, P_HERE, moments, 0)
    for c in m_copies:
        c.wait_recv()

    rims = edges(u_pos, u_neg, cells(mom_lo, 2), cells(mom_lo, 3), cells(mom_hi, 0), cells(mom_hi, 1))
    for x in range(WX):
        part[:, x * WY:(x + 1) * WY] += rims[x]
    s_copy.start()

    outs = [pltpu.make_async_copy(acc.at[pl.ds(p * 400, 400)], out_hbm.at[pl.ds(p * 400, 400)], out_sem.at[p])
            for p in range(P_HERE)]
    outs.append(pltpu.make_async_copy(stress, stress_hbm, out_sem.at[P_HERE]))
    for p in range(P_HERE):
        if p == LAST:
            s_copy.wait_recv()
            total = part[...] + part_other[...]
            for x in range(WX):
                stress[:, x, :] = cells(total, x)[0:3]
            outs[P_HERE].start()
        for c in x_copies[p]:
            c.wait_recv()
        add = rim_terms(vel, recv_lo, recv_hi, p)
        for x in range(WX):
            acc[pl.ds(p * 400 + x, QR, stride=WX), :] += add[x]
        outs[p].start()
    for pair in x_copies + [z_copies, m_copies, (col_copy, s_copy)]:
        for c in pair:
            c.wait_send()
    for c in outs:
        c.wait()


def hand_on(made, made_stress, out, stress, sem):
    copies = [pltpu.make_async_copy(made.at[pl.ds(p * 400, 400)], out.at[pl.ds(p * 400, 400)], sem.at[p])
              for p in range(P_HERE)]
    copies.append(pltpu.make_async_copy(made_stress, stress, sem.at[P_HERE]))
    for c in copies:
        c.start()
    for c in copies:
        c.wait()


def body(nx, ny, density, velocity, shear_rates, hermite_matrix, laguerre_matrix, flow_first,
         flow_second, stress_weights):
    assert density.shape == (P_HERE, HM, HM, WX, WY)
    f32, bf16 = jnp.float32, jnp.bfloat16
    hbm = pl.BlockSpec(memory_space=pltpu.HBM)
    dma = pltpu.SemaphoreType.DMA
    whole, half = (ROWS, WY), (ROWS // 2, WY)
    rims, sums = (8 * GROUPS, WY), (8, WX * WY)
    flows = (4 * HM, HM)
    results = (jax.ShapeDtypeStruct(whole, f32), jax.ShapeDtypeStruct((3, WX, WY), f32))
    params = functools.partial(pltpu.CompilerParams, vmem_limit_bytes=60 * 1024 * 1024)
    made = pl.pallas_call(
        functools.partial(kernel, nx, ny),
        out_shape=results,
        in_specs=[hbm] * 8,
        out_specs=(hbm, hbm),
        scratch_shapes=[
            pltpu.VMEM(whole, f32), pltpu.VMEM(half, f32), pltpu.VMEM(half, f32),
            pltpu.VMEM(sums, f32), pltpu.VMEM(sums, f32), pltpu.VMEM((3, WX, WY), f32),
            pltpu.VMEM(whole, f32), pltpu.VMEM(whole, f32),
            pltpu.VMEM((2, WX, WY), f32), pltpu.VMEM((4, WX, WY), f32),
            pltpu.VMEM((HM, HM), f32), pltpu.VMEM((HM, HM), f32),
            pltpu.VMEM(flows, f32), pltpu.VMEM(flows, f32),
            pltpu.VMEM((P_HERE, HM, 3, HM), f32), pltpu.VMEM((P_HERE * HM * 8, HM), f32),
            pltpu.VMEM((P_HERE, 8, QR), f32),
            pltpu.VMEM(half, f32), pltpu.VMEM(half, f32),
            pltpu.VMEM(rims, f32), pltpu.VMEM(rims, f32), pltpu.VMEM(rims, f32),
            pltpu.VMEM((2 * PQ, WX * WY), f32), pltpu.VMEM((WR, 2 * PQ), bf16), pltpu.VMEM((WR, 2 * PQ), bf16),
            pltpu.VMEM((QR, QR), bf16), pltpu.VMEM((QR, QR), bf16),
            pltpu.VMEM(sums, f32), pltpu.VMEM(sums, f32), pltpu.VMEM(sums, f32),
            dma((P_HERE,)), dma((7,)), dma((P_HERE + 1,)), dma((2, P_HERE)), dma((2, P_HERE)), dma((2,)),
            dma((2,)), dma((2,)), dma((2,)), dma((2,)), dma((2,)),
        ],
        compiler_params=params(collective_id=0, has_side_effects=True),
        cost_estimate=pl.CostEstimate(flops=600_000_000, bytes_accessed=3_000_000, transcendentals=0),
    )(
        density.reshape(whole), velocity, shear_rates, hermite_matrix, laguerre_matrix,
        flow_first.transpose(1, 0, 2).reshape(flows), flow_second.transpose(1, 0, 2).reshape(flows),
        stress_weights.transpose(1, 2, 0, 3),
    )
    advanced, stress = pl.pallas_call(
        hand_on,
        out_shape=results,
        in_specs=[hbm, hbm],
        out_specs=(hbm, hbm),
        scratch_shapes=[dma((P_HERE + 1,))],
        compiler_params=params(),
        cost_estimate=pl.CostEstimate(flops=0, bytes_accessed=2_000_000, transcendentals=0),
    )(*made)
    return advanced.reshape(density.shape), stress


def solution(mesh):
    in_specs = (
        P("col", None, None, "gx", "gy"),
        P(None, "gx", "gy"),
        P(None, "gx", "gy"),
        P(),
        P(),
        P(),
        P(),
        P(None, "col", None, None),
    )
    out_specs = (P("col", None, None, "gx", "gy"), P(None, "gx", "gy"))
    one_device = functools.partial(body, mesh.shape["gx"], mesh.shape["gy"])
    return jax.shard_map(one_device, mesh=mesh, in_specs=in_specs, out_specs=out_specs, check_vma=False)
```

```python
import functools

import jax
import jax.numpy as jnp
from jax import lax
from jax.experimental import pallas as pl
from jax.experimental.pallas import tpu as pltpu
from jax.sharding import PartitionSpec as P

time_step = 0.1
highest = lax.Precision.HIGHEST
MESH = pl.DeviceIdType.MESH

P_HERE = 5
HM = 10
QR = 100
WX = 4
WY = 128
ROWS = P_HERE * QR * WX
PQ = 56
WR = 288
GROUPS, PER = 10, 25
EARLY = 4
LAST = P_HERE - 1


def dot(a, b):
    return jnp.dot(a, b, precision=highest, preferred_element_type=jnp.float32)


def tenth(i):
    return lax.shift_right_logical(i * 205, 11)


def iota(shape, axis):
    return lax.broadcasted_iota(jnp.int32, shape, axis)


def one(cond):
    return jnp.where(cond, 1.0, 0.0).astype(jnp.float32)


def halves(a):
    hi = a.astype(jnp.bfloat16)
    return hi, (a - hi.astype(jnp.float32)).astype(jnp.bfloat16)


def dot3(a_hi, a_lo, b):
    b_hi, b_lo = halves(b)
    mul = functools.partial(jnp.dot, preferred_element_type=jnp.float32)
    return mul(a_hi, b_hi) + (mul(a_hi, b_lo) + mul(a_lo, b_hi))


def cells(tile, x):
    return tile[:, x * WY:(x + 1) * WY]


def speeds(vel):
    u_pos = [-time_step * jnp.maximum(vel[0, x:x + 1, :], 0.0) for x in range(WX)]
    u_neg = [-time_step * jnp.minimum(vel[0, x:x + 1, :], 0.0) for x in range(WX)]
    return u_pos, u_neg


def edges(u_pos, u_neg, lo2, lo1, hi0, hi1):
    return ((-2.0 * u_pos[0]) * lo1 + (0.5 * u_pos[0]) * lo2,
            (0.5 * u_pos[1]) * lo1,
            (-0.5 * u_neg[2]) * hi0,
            (2.0 * u_neg[3]) * hi0 + (-0.5 * u_neg[3]) * hi1)


def rim_terms(vel, recv_lo, recv_hi, p):
    lo2, lo1 = (recv_lo[pl.ds(p * 200 + j, QR, stride=2), :] for j in range(2))
    hi0, hi1 = (recv_hi[pl.ds(p * 200 + j, QR, stride=2), :] for j in range(2))
    return edges(*speeds(vel), lo2, lo1, hi0, hi1)


def kernel(nx, ny, dens_hbm, vel_hbm, shear_hbm, herm_hbm, lag_hbm, ff_hbm, fs_hbm, sw_hbm,
           out_hbm, stress_hbm,
           acc, recv_lo, recv_hi, part, part_other, stress, dens, other, vel, shear, herm, lag, ff, fs, sw_in, sw_rows, sw,
           send_lo, send_hi, rim, rim_lo, rim_hi,
           xs, w_hi, w_lo, kqr_hi, kqr_lo, mom, mom_lo, mom_hi,
           load_sem, in_sem, out_sem, xs_send, xs_recv, col_sem, z_send, z_recv, m_send, m_recv, s_sem):
    gx, gy, col = lax.axis_index("gx"), lax.axis_index("gy"), lax.axis_index("col")
    x_next, x_prev = lax.rem(gx + 1, nx), lax.rem(gx + nx - 1, nx)
    y_next, y_prev = lax.rem(gy + 1, ny), lax.rem(gy + ny - 1, ny)
    to_next, to_prev = (x_next, gy, col), (x_prev, gy, col)
    to_up, to_down = (gx, y_next, col), (gx, y_prev, col)
    to_col = (gx, gy, 1 - col)

    loads = [pltpu.make_async_copy(dens_hbm.at[pl.ds(p * 400, 400)], dens.at[pl.ds(p * 400, 400)],
                                   load_sem.at[p]) for p in range(P_HERE)]
    smalls = [pltpu.make_async_copy(src, dst, in_sem.at[i]) for i, (src, dst) in enumerate((
        (vel_hbm, vel), (herm_hbm, herm), (lag_hbm, lag), (sw_hbm, sw_in),
        (ff_hbm, ff), (fs_hbm, fs), (shear_hbm, shear)))]
    for c in loads + smalls:
        c.start()
    barrier = pltpu.get_barrier_semaphore()
    for d in (to_next, to_prev, to_up, to_down, to_col):
        pl.semaphore_signal(barrier, inc=1, device_id=d, device_id_type=MESH)

    def remote(src, dst, ss, rs, dev):
        return pltpu.make_async_remote_copy(src_ref=src, dst_ref=dst, send_sem=ss, recv_sem=rs,
                                            device_id=dev, device_id_type=MESH)

    x_copies = []
    for p in range(P_HERE):
        piece = pl.ds(p * 200, 200)
        x_copies.append((
            remote(send_hi.at[piece], recv_lo.at[piece], xs_send.at[0, p], xs_recv.at[0, p], to_next),
            remote(send_lo.at[piece], recv_hi.at[piece], xs_send.at[1, p], xs_recv.at[1, p], to_prev)))
    col_copy = remote(dens, other, col_sem.at[0], col_sem.at[1], to_col)
    z_copies = (remote(rim, rim_lo, z_send.at[0], z_recv.at[0], to_up),
                remote(rim, rim_hi, z_send.at[1], z_recv.at[1], to_down))
    m_copies = (remote(mom, mom_lo, m_send.at[0], m_recv.at[0], to_next),
                remote(mom, mom_hi, m_send.at[1], m_recv.at[1], to_prev))
    s_copy = remote(part, part_other, s_sem.at[0], s_sem.at[1], to_col)

    for p in range(P_HERE):
        loads[p].wait()
        for j in range(2):
            rows = pl.ds(p * 200 + j, QR, stride=2)
            send_lo[rows, :] = dens[pl.ds(p * 400 + j, QR, stride=WX), :]
            send_hi[rows, :] = dens[pl.ds(p * 400 + 2 + j, QR, stride=WX), :]
        if p == 0:
            pl.semaphore_wait(barrier, 5)
        if p < EARLY:
            for c in x_copies[p]:
                c.start()
    col_copy.start()

    lane = iota((8, WY), 1)

    def pack(g, _):
        tile = jnp.zeros((8, WY), jnp.float32)
        for k in range(PER):
            f = dens[pl.ds(pl.multiple_of(g * (8 * PER), 8) + 8 * k, 8), :]
            tile = jnp.where((lane >> 2) == k, pltpu.roll(f, (4 * k + 2) % WY, 1), tile)
        rim[pl.ds(pl.multiple_of(g * 8, 8), 8), :] = tile
        return 0

    lax.fori_loop(0, GROUPS, pack, 0)
    for c in z_copies:
        c.start()

    for c in smalls:
        c.wait()
    sw_rows[...] = jnp.zeros_like(sw_rows)
    for p in range(P_HERE):
        for q in range(HM):
            at = (p * HM + q) * 8
            sw_rows[at:at + 3, :] = sw_in[p, q]
    lane_qr = iota((8, QR), 1)
    q_of, r_hot = tenth(lane_qr), iota((HM, QR), 1)
    spread = dot(sw_rows[...], one(r_hot - 10 * tenth(r_hot) == iota((HM, QR), 0)))
    for p in range(P_HERE):
        sw[p] = sum(jnp.where(q_of == q, spread[(p * HM + q) * 8:(p * HM + q) * 8 + 8], 0.0) for q in range(HM))

    row, hot = iota((QR, HM), 0), iota((QR, HM), 1)
    row_t, hot_t = iota((HM, QR), 1), iota((HM, QR), 0)
    rr, cc = iota((QR, QR), 0), iota((QR, QR), 1)
    rq, cq = tenth(rr), tenth(cc)
    h_exp = dot(dot(one(tenth(row) == hot), herm[...]), one(tenth(row_t) == hot_t))
    l_exp = dot(dot(one(row - 10 * tenth(row) == hot), lag[...]), one(row_t - 10 * tenth(row_t) == hot_t))
    kqr_hi[...], kqr_lo[...] = halves(time_step * (jnp.where(rr - 10 * rq == cc - 10 * cq, h_exp, 0.0) + jnp.where(rq == cq, l_exp, 0.0)))

    u_pos, u_neg = speeds(vel)

    mom[...] = jnp.zeros_like(mom)

    def own(p, _):
        c = [dens[pl.ds(p * 400 + x, QR, stride=WX), :] for x in range(WX)]
        block = jnp.concatenate(c, axis=1)
        rate = dot3(kqr_hi[...], kqr_lo[...], block)
        mom[...] += dot(sw[p], block)
        for x in range(WX):
            value = cells(rate, x) + (1.5 * (u_pos[x] - u_neg[x])) * c[x]
            if x >= 1:
                value += (-2.0 * u_pos[x]) * c[x - 1]
            if x >= 2:
                value += (0.5 * u_pos[x]) * c[x - 2]
            if x < WX - 1:
                value += (2.0 * u_neg[x]) * c[x + 1]
            if x < WX - 2:
                value += (-0.5 * u_neg[x]) * c[x + 2]
            acc[pl.ds(p * 400 + x, QR, stride=WX), :] = value
        return 0

    lax.fori_loop(0, P_HERE, own, 0)
    for c in m_copies:
        c.start()
    for p in range(EARLY, P_HERE):
        for c in x_copies[p]:
            c.start()

    my0, other0 = col * P_HERE, (1 - col) * P_HERE
    r1, k1 = iota((WR, 50), 0), iota((WR, 50), 1)
    comp = sum(jnp.where(r1 >= PQ * c, 1, 0) for c in range(1, 5))
    r1 = jnp.where(r1 < 5 * PQ, r1 - PQ * comp, PQ)
    flow, a_of = comp < 4, tenth(r1)
    b_of = r1 - 10 * a_of
    a_hot = one((r1 < 50) & (k1 == jnp.where(flow, 4 * (my0 + a_of) + comp, 40 + my0 + a_of)))
    b_hot = one((r1 < 50) & (k1 == jnp.where(flow, 4 * b_of + comp, 40 + b_of)))
    c2, j2 = iota((HM, 2 * PQ), 1), iota((HM, 2 * PQ), 0)
    near = c2 < PQ
    c2 = jnp.where(near, c2, c2 - PQ)
    real = c2 < 50
    p_hot = one(real & (j2 == jnp.where(near, my0, other0) + tenth(c2)))
    q_hot = one(real & (j2 == c2 - 10 * tenth(c2)))
    eye = one(iota((HM, HM), 0) == iota((HM, HM), 1))
    first = dot(dot(a_hot, jnp.concatenate([ff[...], herm[...]], axis=0)), p_hot)
    second = dot(dot(b_hot, jnp.concatenate([fs[...], eye], axis=0)), q_hot)
    w_hi[...], w_lo[...] = halves(time_step * first * second)
    xs[...] = jnp.zeros_like(xs)

    for c in z_copies:
        c.wait_recv()
    v = jnp.concatenate([vel[1], vel[1]], axis=0)
    v_pos = -time_step * jnp.maximum(v, 0.0)
    v_neg = -time_step * jnp.minimum(v, 0.0)
    k_0 = 1.0 + 1.5 * (v_pos - v_neg)
    k_m1, k_m2, k_p1, k_p2 = -2.0 * v_pos, 0.5 * v_pos, 2.0 * v_neg, -0.5 * v_neg
    low_wall = jnp.where(gy == 0, 0.0, 1.0).astype(jnp.float32)
    high_wall = jnp.where(gy == ny - 1, 0.0, 1.0).astype(jnp.float32)

    def normal(g, _):
        at = pl.ds(pl.multiple_of(g * 8, 8), 8)
        rims = jnp.where((lane & 3) < 2, rim_lo[at, :] * low_wall, rim_hi[at, :] * high_wall)
        for k in range(PER):
            here = pl.ds(pl.multiple_of(g * (8 * PER), 8) + 8 * k, 8)
            f = dens[here, :]
            h = pltpu.roll(rims, (2 * WY - 4 * k - 2) % WY, 1)
            m1 = pltpu.roll(jnp.where(lane == WY - 1, h, f), 1, 1)
            m2 = pltpu.roll(jnp.where(lane >= WY - 2, h, f), 2, 1)
            p1 = pltpu.roll(jnp.where(lane == 0, h, f), WY - 1, 1)
            p2 = pltpu.roll(jnp.where(lane < 2, h, f), WY - 2, 1)
            acc[here, :] += k_0 * f + k_m1 * m1 + k_m2 * m2 + k_p1 * p1 + k_p2 * p2
        return 0

    lax.fori_loop(0, GROUPS, normal, 0)

    col_copy.wait_recv()

    def couple(r, _):
        for x in range(WX):
            rows = pl.ds(r * WX + x, 50, stride=40)
            xs[0:50, x * WY:(x + 1) * WY] = dens[rows, :]
            xs[PQ:PQ + 50, x * WY:(x + 1) * WY] = other[rows, :]
        t = dot3(w_hi[...], w_lo[...], xs[...])
        for x in range(WX):
            value = cells(t, x)[4 * PQ:4 * PQ + 50]
            for c in range(4):
                value += shear[c, x:x + 1, :] * cells(t, x)[c * PQ:c * PQ + 50]
            acc[pl.ds(r * WX + x, 50, stride=40), :] += value
        return 0

    lax.fori_loop(0, HM, couple, 0)

    part[...] = jnp.zeros_like(part)

    def moments(p, _):
        block = jnp.concatenate([acc[pl.ds(p * 400 + x, QR, stride=WX), :] for x in range(WX)], axis=1)
        part[...] += dot(sw[p], block)
        return 0

    lax.fori_loop(0, P_HERE, moments, 0)
    for c in m_copies:
        c.wait_recv()

    rims = edges(u_pos, u_neg, cells(mom_lo, 2), cells(mom_lo, 3), cells(mom_hi, 0), cells(mom_hi, 1))
    for x in range(WX):
        part[:, x * WY:(x + 1) * WY] += rims[x]
    s_copy.start()

    outs = [pltpu.make_async_copy(acc.at[pl.ds(p * 400, 400)], out_hbm.at[pl.ds(p * 400, 400)], out_sem.at[p])
            for p in range(P_HERE)]
    outs.append(pltpu.make_async_copy(stress, stress_hbm, out_sem.at[P_HERE]))
    for p in range(P_HERE):
        if p == LAST:
            s_copy.wait_recv()
            total = part[...] + part_other[...]
            for x in range(WX):
                stress[:, x, :] = cells(total, x)[0:3]
            outs[P_HERE].start()
        for c in x_copies[p]:
            c.wait_recv()
        add = rim_terms(vel, recv_lo, recv_hi, p)
        for x in range(WX):
            acc[pl.ds(p * 400 + x, QR, stride=WX), :] += add[x]
        outs[p].start()
    for pair in x_copies + [z_copies, m_copies, (col_copy, s_copy)]:
        for c in pair:
            c.wait_send()
    for c in outs:
        c.wait()


def body(nx, ny, density, velocity, shear_rates, hermite_matrix, laguerre_matrix, flow_first,
         flow_second, stress_weights):
    assert density.shape == (P_HERE, HM, HM, WX, WY)
    f32, bf16 = jnp.float32, jnp.bfloat16
    hbm = pl.BlockSpec(memory_space=pltpu.HBM)
    dma = pltpu.SemaphoreType.DMA
    whole, half = (ROWS, WY), (ROWS // 2, WY)
    rims, sums = (8 * GROUPS, WY), (8, WX * WY)
    flows = (4 * HM, HM)
    results = (jax.ShapeDtypeStruct(whole, f32), jax.ShapeDtypeStruct((3, WX, WY), f32))
    advanced, stress = pl.pallas_call(
        functools.partial(kernel, nx, ny),
        out_shape=results,
        in_specs=[hbm] * 8,
        out_specs=(hbm, hbm),
        scratch_shapes=[
            pltpu.VMEM(whole, f32), pltpu.VMEM(half, f32), pltpu.VMEM(half, f32),
            pltpu.VMEM(sums, f32), pltpu.VMEM(sums, f32), pltpu.VMEM((3, WX, WY), f32),
            pltpu.VMEM(whole, f32), pltpu.VMEM(whole, f32),
            pltpu.VMEM((2, WX, WY), f32), pltpu.VMEM((4, WX, WY), f32),
            pltpu.VMEM((HM, HM), f32), pltpu.VMEM((HM, HM), f32),
            pltpu.VMEM(flows, f32), pltpu.VMEM(flows, f32),
            pltpu.VMEM((P_HERE, HM, 3, HM), f32), pltpu.VMEM((P_HERE * HM * 8, HM), f32),
            pltpu.VMEM((P_HERE, 8, QR), f32),
            pltpu.VMEM(half, f32), pltpu.VMEM(half, f32),
            pltpu.VMEM(rims, f32), pltpu.VMEM(rims, f32), pltpu.VMEM(rims, f32),
            pltpu.VMEM((2 * PQ, WX * WY), f32), pltpu.VMEM((WR, 2 * PQ), bf16), pltpu.VMEM((WR, 2 * PQ), bf16),
            pltpu.VMEM((QR, QR), bf16), pltpu.VMEM((QR, QR), bf16),
            pltpu.VMEM(sums, f32), pltpu.VMEM(sums, f32), pltpu.VMEM(sums, f32),
            dma((P_HERE,)), dma((7,)), dma((P_HERE + 1,)), dma((2, P_HERE)), dma((2, P_HERE)), dma((2,)),
            dma((2,)), dma((2,)), dma((2,)), dma((2,)), dma((2,)),
        ],
        compiler_params=pltpu.CompilerParams(collective_id=0, has_side_effects=True,
                                             vmem_limit_bytes=60 * 1024 * 1024),
        cost_estimate=pl.CostEstimate(flops=600_000_000, bytes_accessed=3_000_000, transcendentals=0),
    )(
        density.reshape(whole), velocity, shear_rates, hermite_matrix, laguerre_matrix,
        flow_first.transpose(1, 0, 2).reshape(flows), flow_second.transpose(1, 0, 2).reshape(flows),
        stress_weights.transpose(1, 2, 0, 3),
    )
    return advanced.reshape(density.shape), stress


def solution(mesh):
    in_specs = (
        P("col", None, None, "gx", "gy"),
        P(None, "gx", "gy"),
        P(None, "gx", "gy"),
        P(),
        P(),
        P(),
        P(),
        P(None, "col", None, None),
    )
    out_specs = (P("col", None, None, "gx", "gy"), P(None, "gx", "gy"))
    one_device = functools.partial(body, mesh.shape["gx"], mesh.shape["gy"])
    return jax.shard_map(one_device, mesh=mesh, in_specs=in_specs, out_specs=out_specs, check_vma=False)
```

```python
import functools

import jax
import jax.numpy as jnp
from jax import lax
from jax.experimental import pallas as pl
from jax.experimental.pallas import tpu as pltpu
from jax.sharding import PartitionSpec as P

time_step = 0.1
highest = lax.Precision.HIGHEST
MESH = pl.DeviceIdType.MESH

P_HERE = 5
HM = 10
QR = 100
WX = 4
WY = 128
ROWS = P_HERE * QR * WX
PQ = 56
WR = 288
GROUPS, PER = 10, 25
EARLY = 4
LAST = P_HERE - 1


def dot(a, b):
    return jnp.dot(a, b, precision=highest, preferred_element_type=jnp.float32)


def tenth(i):
    return lax.shift_right_logical(i * 205, 11)


def iota(shape, axis):
    return lax.broadcasted_iota(jnp.int32, shape, axis)


def one(cond):
    return jnp.where(cond, 1.0, 0.0).astype(jnp.float32)


def halves(a):
    hi = a.astype(jnp.bfloat16)
    return hi, (a - hi.astype(jnp.float32)).astype(jnp.bfloat16)


def dot3(a_hi, a_lo, b):
    b_hi, b_lo = halves(b)
    mul = functools.partial(jnp.dot, preferred_element_type=jnp.float32)
    return mul(a_hi, b_hi) + (mul(a_hi, b_lo) + mul(a_lo, b_hi))


def cells(tile, x):
    return tile[:, x * WY:(x + 1) * WY]


def speeds(vel):
    u_pos = [-time_step * jnp.maximum(vel[0, x:x + 1, :], 0.0) for x in range(WX)]
    u_neg = [-time_step * jnp.minimum(vel[0, x:x + 1, :], 0.0) for x in range(WX)]
    return u_pos, u_neg


def edges(u_pos, u_neg, lo2, lo1, hi0, hi1):
    return ((-2.0 * u_pos[0]) * lo1 + (0.5 * u_pos[0]) * lo2,
            (0.5 * u_pos[1]) * lo1,
            (-0.5 * u_neg[2]) * hi0,
            (2.0 * u_neg[3]) * hi0 + (-0.5 * u_neg[3]) * hi1)


def rim_terms(vel, recv_lo, recv_hi, p):
    lo2, lo1 = (recv_lo[pl.ds(p * 200 + j, QR, stride=2), :] for j in range(2))
    hi0, hi1 = (recv_hi[pl.ds(p * 200 + j, QR, stride=2), :] for j in range(2))
    return edges(*speeds(vel), lo2, lo1, hi0, hi1)


def kernel(nx, ny, dens_hbm, vel_hbm, shear_hbm, herm_hbm, lag_hbm, ff_hbm, fs_hbm, sw_hbm,
           acc, stress,
           recv_lo, recv_hi, part, part_other, dens, other, vel, shear, herm, lag, ff, fs, sw_in, sw_rows, sw,
           send_lo, send_hi, rim, rim_lo, rim_hi,
           xs, w_hi, w_lo, kqr_hi, kqr_lo, mom, mom_lo, mom_hi,
           load_sem, in_sem, xs_send, xs_recv, col_sem, z_send, z_recv, m_send, m_recv, s_sem):
    gx, gy, col = lax.axis_index("gx"), lax.axis_index("gy"), lax.axis_index("col")
    x_next, x_prev = lax.rem(gx + 1, nx), lax.rem(gx + nx - 1, nx)
    y_next, y_prev = lax.rem(gy + 1, ny), lax.rem(gy + ny - 1, ny)
    to_next, to_prev = (x_next, gy, col), (x_prev, gy, col)
    to_up, to_down = (gx, y_next, col), (gx, y_prev, col)
    to_col = (gx, gy, 1 - col)

    loads = [pltpu.make_async_copy(dens_hbm.at[pl.ds(p * 400, 400)], dens.at[pl.ds(p * 400, 400)],
                                   load_sem.at[p]) for p in range(P_HERE)]
    smalls = [pltpu.make_async_copy(src, dst, in_sem.at[i]) for i, (src, dst) in enumerate((
        (vel_hbm, vel), (herm_hbm, herm), (lag_hbm, lag), (sw_hbm, sw_in),
        (ff_hbm, ff), (fs_hbm, fs), (shear_hbm, shear)))]
    for c in loads + smalls:
        c.start()
    barrier = pltpu.get_barrier_semaphore()
    for d in (to_next, to_prev, to_up, to_down, to_col):
        pl.semaphore_signal(barrier, inc=1, device_id=d, device_id_type=MESH)

    def remote(src, dst, ss, rs, dev):
        return pltpu.make_async_remote_copy(src_ref=src, dst_ref=dst, send_sem=ss, recv_sem=rs,
                                            device_id=dev, device_id_type=MESH)

    x_copies = []
    for p in range(P_HERE):
        piece = pl.ds(p * 200, 200)
        x_copies.append((
            remote(send_hi.at[piece], recv_lo.at[piece], xs_send.at[0, p], xs_recv.at[0, p], to_next),
            remote(send_lo.at[piece], recv_hi.at[piece], xs_send.at[1, p], xs_recv.at[1, p], to_prev)))
    col_copy = remote(dens, other, col_sem.at[0], col_sem.at[1], to_col)
    z_copies = (remote(rim, rim_lo, z_send.at[0], z_recv.at[0], to_up),
                remote(rim, rim_hi, z_send.at[1], z_recv.at[1], to_down))
    m_copies = (remote(mom, mom_lo, m_send.at[0], m_recv.at[0], to_next),
                remote(mom, mom_hi, m_send.at[1], m_recv.at[1], to_prev))
    s_copy = remote(part, part_other, s_sem.at[0], s_sem.at[1], to_col)

    for p in range(P_HERE):
        loads[p].wait()
        for j in range(2):
            rows = pl.ds(p * 200 + j, QR, stride=2)
            send_lo[rows, :] = dens[pl.ds(p * 400 + j, QR, stride=WX), :]
            send_hi[rows, :] = dens[pl.ds(p * 400 + 2 + j, QR, stride=WX), :]
        if p == 0:
            pl.semaphore_wait(barrier, 5)
        if p < EARLY:
            for c in x_copies[p]:
                c.start()
    col_copy.start()

    lane = iota((8, WY), 1)

    def pack(g, _):
        tile = jnp.zeros((8, WY), jnp.float32)
        for k in range(PER):
            f = dens[pl.ds(pl.multiple_of(g * (8 * PER), 8) + 8 * k, 8), :]
            tile = jnp.where((lane >> 2) == k, pltpu.roll(f, (4 * k + 2) % WY, 1), tile)
        rim[pl.ds(pl.multiple_of(g * 8, 8), 8), :] = tile
        return 0

    lax.fori_loop(0, GROUPS, pack, 0)
    for c in z_copies:
        c.start()

    for c in smalls:
        c.wait()
    sw_rows[...] = jnp.zeros_like(sw_rows)
    for p in range(P_HERE):
        for q in range(HM):
            at = (p * HM + q) * 8
            sw_rows[at:at + 3, :] = sw_in[p, q]
    lane_qr = iota((8, QR), 1)
    q_of, r_hot = tenth(lane_qr), iota((HM, QR), 1)
    spread = dot(sw_rows[...], one(r_hot - 10 * tenth(r_hot) == iota((HM, QR), 0)))
    for p in range(P_HERE):
        sw[p] = sum(jnp.where(q_of == q, spread[(p * HM + q) * 8:(p * HM + q) * 8 + 8], 0.0) for q in range(HM))

    row, hot = iota((QR, HM), 0), iota((QR, HM), 1)
    row_t, hot_t = iota((HM, QR), 1), iota((HM, QR), 0)
    rr, cc = iota((QR, QR), 0), iota((QR, QR), 1)
    rq, cq = tenth(rr), tenth(cc)
    h_exp = dot(dot(one(tenth(row) == hot), herm[...]), one(tenth(row_t) == hot_t))
    l_exp = dot(dot(one(row - 10 * tenth(row) == hot), lag[...]), one(row_t - 10 * tenth(row_t) == hot_t))
    kqr_hi[...], kqr_lo[...] = halves(time_step * (jnp.where(rr - 10 * rq == cc - 10 * cq, h_exp, 0.0) + jnp.where(rq == cq, l_exp, 0.0)))

    u_pos, u_neg = speeds(vel)

    mom[...] = jnp.zeros_like(mom)

    def own(p, _):
        c = [dens[pl.ds(p * 400 + x, QR, stride=WX), :] for x in range(WX)]
        block = jnp.concatenate(c, axis=1)
        rate = dot3(kqr_hi[...], kqr_lo[...], block)
        mom[...] += dot(sw[p], block)
        for x in range(WX):
            value = cells(rate, x) + (1.5 * (u_pos[x] - u_neg[x])) * c[x]
            if x >= 1:
                value += (-2.0 * u_pos[x]) * c[x - 1]
            if x >= 2:
                value += (0.5 * u_pos[x]) * c[x - 2]
            if x < WX - 1:
                value += (2.0 * u_neg[x]) * c[x + 1]
            if x < WX - 2:
                value += (-0.5 * u_neg[x]) * c[x + 2]
            acc[pl.ds(p * 400 + x, QR, stride=WX), :] = value
        return 0

    lax.fori_loop(0, P_HERE, own, 0)
    for c in m_copies:
        c.start()
    for p in range(EARLY, P_HERE):
        for c in x_copies[p]:
            c.start()

    my0, other0 = col * P_HERE, (1 - col) * P_HERE
    r1, k1 = iota((WR, 50), 0), iota((WR, 50), 1)
    comp = sum(jnp.where(r1 >= PQ * c, 1, 0) for c in range(1, 5))
    r1 = jnp.where(r1 < 5 * PQ, r1 - PQ * comp, PQ)
    flow, a_of = comp < 4, tenth(r1)
    b_of = r1 - 10 * a_of
    a_hot = one((r1 < 50) & (k1 == jnp.where(flow, 4 * (my0 + a_of) + comp, 40 + my0 + a_of)))
    b_hot = one((r1 < 50) & (k1 == jnp.where(flow, 4 * b_of + comp, 40 + b_of)))
    c2, j2 = iota((HM, 2 * PQ), 1), iota((HM, 2 * PQ), 0)
    near = c2 < PQ
    c2 = jnp.where(near, c2, c2 - PQ)
    real = c2 < 50
    p_hot = one(real & (j2 == jnp.where(near, my0, other0) + tenth(c2)))
    q_hot = one(real & (j2 == c2 - 10 * tenth(c2)))
    eye = one(iota((HM, HM), 0) == iota((HM, HM), 1))
    first = dot(dot(a_hot, jnp.concatenate([ff[...], herm[...]], axis=0)), p_hot)
    second = dot(dot(b_hot, jnp.concatenate([fs[...], eye], axis=0)), q_hot)
    w_hi[...], w_lo[...] = halves(time_step * first * second)
    xs[...] = jnp.zeros_like(xs)

    for c in z_copies:
        c.wait_recv()
    v = jnp.concatenate([vel[1], vel[1]], axis=0)
    v_pos = -time_step * jnp.maximum(v, 0.0)
    v_neg = -time_step * jnp.minimum(v, 0.0)
    k_0 = 1.0 + 1.5 * (v_pos - v_neg)
    k_m1, k_m2, k_p1, k_p2 = -2.0 * v_pos, 0.5 * v_pos, 2.0 * v_neg, -0.5 * v_neg
    low_wall = jnp.where(gy == 0, 0.0, 1.0).astype(jnp.float32)
    high_wall = jnp.where(gy == ny - 1, 0.0, 1.0).astype(jnp.float32)

    def normal(g, _):
        at = pl.ds(pl.multiple_of(g * 8, 8), 8)
        rims = jnp.where((lane & 3) < 2, rim_lo[at, :] * low_wall, rim_hi[at, :] * high_wall)
        for k in range(PER):
            here = pl.ds(pl.multiple_of(g * (8 * PER), 8) + 8 * k, 8)
            f = dens[here, :]
            h = pltpu.roll(rims, (2 * WY - 4 * k - 2) % WY, 1)
            m1 = pltpu.roll(jnp.where(lane == WY - 1, h, f), 1, 1)
            m2 = pltpu.roll(jnp.where(lane >= WY - 2, h, f), 2, 1)
            p1 = pltpu.roll(jnp.where(lane == 0, h, f), WY - 1, 1)
            p2 = pltpu.roll(jnp.where(lane < 2, h, f), WY - 2, 1)
            acc[here, :] += k_0 * f + k_m1 * m1 + k_m2 * m2 + k_p1 * p1 + k_p2 * p2
        return 0

    lax.fori_loop(0, GROUPS, normal, 0)

    col_copy.wait_recv()

    def couple(r, _):
        for x in range(WX):
            rows = pl.ds(r * WX + x, 50, stride=40)
            xs[0:50, x * WY:(x + 1) * WY] = dens[rows, :]
            xs[PQ:PQ + 50, x * WY:(x + 1) * WY] = other[rows, :]
        t = dot3(w_hi[...], w_lo[...], xs[...])
        for x in range(WX):
            value = cells(t, x)[4 * PQ:4 * PQ + 50]
            for c in range(4):
                value += shear[c, x:x + 1, :] * cells(t, x)[c * PQ:c * PQ + 50]
            acc[pl.ds(r * WX + x, 50, stride=40), :] += value
        return 0

    lax.fori_loop(0, HM, couple, 0)

    part[...] = jnp.zeros_like(part)

    def moments(p, _):
        block = jnp.concatenate([acc[pl.ds(p * 400 + x, QR, stride=WX), :] for x in range(WX)], axis=1)
        part[...] += dot(sw[p], block)
        return 0

    lax.fori_loop(0, P_HERE, moments, 0)
    for c in m_copies:
        c.wait_recv()

    rims = edges(u_pos, u_neg, cells(mom_lo, 2), cells(mom_lo, 3), cells(mom_hi, 0), cells(mom_hi, 1))
    for x in range(WX):
        part[:, x * WY:(x + 1) * WY] += rims[x]
    s_copy.start()

    for p in range(P_HERE):
        if p == LAST:
            s_copy.wait_recv()
            total = part[...] + part_other[...]
            for x in range(WX):
                stress[:, x, :] = cells(total, x)[0:3]
        for c in x_copies[p]:
            c.wait_recv()
        add = rim_terms(vel, recv_lo, recv_hi, p)
        for x in range(WX):
            acc[pl.ds(p * 400 + x, QR, stride=WX), :] += add[x]
    for pair in x_copies + [z_copies, m_copies, (col_copy, s_copy)]:
        for c in pair:
            c.wait_send()


def body(nx, ny, density, velocity, shear_rates, hermite_matrix, laguerre_matrix, flow_first,
         flow_second, stress_weights):
    assert density.shape == (P_HERE, HM, HM, WX, WY)
    f32, bf16 = jnp.float32, jnp.bfloat16
    hbm = pl.BlockSpec(memory_space=pltpu.HBM)
    vmem = pl.BlockSpec(memory_space=pltpu.VMEM)
    dma = pltpu.SemaphoreType.DMA
    whole, half = (ROWS, WY), (ROWS // 2, WY)
    rims, sums = (8 * GROUPS, WY), (8, WX * WY)
    flows = (4 * HM, HM)
    results = (pltpu.VMEM(whole, f32), pltpu.VMEM((3, WX, WY), f32))
    advanced, stress = pl.pallas_call(
        functools.partial(kernel, nx, ny),
        out_shape=results,
        in_specs=[hbm] * 8,
        out_specs=(vmem, vmem),
        scratch_shapes=[
            pltpu.VMEM(half, f32), pltpu.VMEM(half, f32), pltpu.VMEM(sums, f32), pltpu.VMEM(sums, f32),
            pltpu.VMEM(whole, f32), pltpu.VMEM(whole, f32),
            pltpu.VMEM((2, WX, WY), f32), pltpu.VMEM((4, WX, WY), f32),
            pltpu.VMEM((HM, HM), f32), pltpu.VMEM((HM, HM), f32),
            pltpu.VMEM(flows, f32), pltpu.VMEM(flows, f32),
            pltpu.VMEM((P_HERE, HM, 3, HM), f32), pltpu.VMEM((P_HERE * HM * 8, HM), f32),
            pltpu.VMEM((P_HERE, 8, QR), f32),
            pltpu.VMEM(half, f32), pltpu.VMEM(half, f32),
            pltpu.VMEM(rims, f32), pltpu.VMEM(rims, f32), pltpu.VMEM(rims, f32),
            pltpu.VMEM((2 * PQ, WX * WY), f32), pltpu.VMEM((WR, 2 * PQ), bf16), pltpu.VMEM((WR, 2 * PQ), bf16),
            pltpu.VMEM((QR, QR), bf16), pltpu.VMEM((QR, QR), bf16),
            pltpu.VMEM(sums, f32), pltpu.VMEM(sums, f32), pltpu.VMEM(sums, f32),
            dma((P_HERE,)), dma((7,)), dma((2, P_HERE)), dma((2, P_HERE)), dma((2,)),
            dma((2,)), dma((2,)), dma((2,)), dma((2,)), dma((2,)),
        ],
        compiler_params=pltpu.CompilerParams(collective_id=0, has_side_effects=True,
                                             vmem_limit_bytes=40 * 1024 * 1024),
        cost_estimate=pl.CostEstimate(flops=600_000_000, bytes_accessed=3_000_000, transcendentals=0),
    )(*(pltpu.with_memory_space_constraint(a, pltpu.HBM) for a in (
        density.reshape(whole), velocity, shear_rates, hermite_matrix, laguerre_matrix,
        flow_first.transpose(1, 0, 2).reshape(flows), flow_second.transpose(1, 0, 2).reshape(flows),
        stress_weights.transpose(1, 2, 0, 3),
    )))
    return advanced.reshape(density.shape), stress


def solution(mesh):
    in_specs = (
        P("col", None, None, "gx", "gy"),
        P(None, "gx", "gy"),
        P(None, "gx", "gy"),
        P(),
        P(),
        P(),
        P(),
        P(None, "col", None, None),
    )
    out_specs = (P("col", None, None, "gx", "gy"), P(None, "gx", "gy"))
    one_device = functools.partial(body, mesh.shape["gx"], mesh.shape["gy"])
    return jax.shard_map(one_device, mesh=mesh, in_specs=in_specs, out_specs=out_specs, check_vma=False)
```
